512 devices in a mesh: ctx: 64 (over z, y_hi, core), head: 8 (over y_lo, x).
Axes of the slice: x: 4, y: 4 (y_hi: 2, y_lo: 2; y = y_hi * 2 + y_lo), z: 16, core: 2. Of those that a mesh axis runs over, the one named last changes fastest.
Arguments:
- query: bfloat16 [8192, 128, 128], P(('ctx', 'head')), may hold values from -6 to 6
- key: bfloat16 [8192, 8, 128], P(('ctx', 'head')), may hold values from -6 to 6
- value: bfloat16 [8192, 8, 128], P(('ctx', 'head')), may hold values from -6 to 6
- out_grad: bfloat16 [8192, 128, 128], P(('ctx', 'head')), may hold values from -6 to 6
- doc_lengths: int32 [16], replicated, may hold values from 1 to 1024, 8192 in all
Outputs:
- attended: bfloat16 [8192, 128, 128], P(('ctx', 'head'))
- query_grad: bfloat16 [8192, 128, 128], P(('ctx', 'head'))
- key_grad: bfloat16 [8192, 8, 128], P(('ctx', 'head'))
- value_grad: bfloat16 [8192, 8, 128], P(('ctx', 'head'))
The draws below stay inside these ranges and needn't reach their ends.
Inputs may be any that keep to these rules, and one draw needn't show every extreme that they name: `doc_lengths`: they sum to 8192; the longest is 1024.
All inputs are finite; a program needn't handle non-finite values.
Results may differ from the reference program's by a relative error of at most 0.039.
Values may be sent and summed in bfloat16 or wider, within the bound.
No kernel may reach another device: no remote copies, remote signals or barrier semaphores. Data moves between devices by JAX's collectives and lax.ppermute only.
A program may use at most 64 MiB of HBM per device.

```python
import math
import jax
import jax.numpy as jnp
import numpy as np
from jax import lax

HEADS = 128
KVH = 8
HD = 128
TOK_DEV = 128
REACH = 8
TOKENS = 8192
MOSTDOC = 1024
NDOCS = 16


def draw_query(key, part):
    key = jax.random.fold_in(key, 11)
    values = jnp.clip(jax.random.normal(key, (TOKENS, HEADS, HD), jnp.float32), -6.0, 6.0)
    return values.astype(jnp.bfloat16)


def draw_key(key, part):
    key = jax.random.fold_in(key, 12)
    values = jnp.clip(jax.random.normal(key, (TOKENS, KVH, HD), jnp.float32), -6.0, 6.0)
    return values.astype(jnp.bfloat16)


def block_scale(stream_key, extent, pieces, smallest, largest):
    def one(dim, shards_of):
        heights = jax.random.uniform(jax.random.fold_in(jax.random.fold_in(stream_key, 6), dim), (shards_of,), jnp.float32, smallest / len(pieces), largest / len(pieces))
        return jnp.repeat(jnp.exp(heights), extent[dim] // shards_of).reshape((-1,) + (1,) * (len(extent) - dim - 1))

    factor_of = one(*pieces[0])
    for cut in pieces[1:]:
        factor_of = factor_of * one(*cut)
    return factor_of


def profile(amount, total, reach, skew):
    loads = [(1 << 20) // math.isqrt(rank ** skew) + 1 for rank in range(2, amount + 1)]
    rest, counts = total - reach - (amount - 1), [1] * (amount - 1)
    while rest > 0:
        movable = [i for i in range(amount - 1) if counts[i] < reach]
        whole, budget = sum([loads[i] for i in movable]), rest
        for i in movable:
            addition = min(reach - counts[i], max(1, budget * loads[i] // whole), rest)
            counts[i] = counts[i] + addition
            rest = rest - addition
    return np.array([reach] + counts)


def uneven_parts(own_key, count, total, limit, slope):
    if count == 2:
        one = jax.random.randint(own_key, (), max(1, total - limit), min(limit, total - 1) + 1)
        return jnp.stack([one, total - one])
    tallies = jnp.asarray(profile(count, total, limit, slope), jnp.int32)
    pairs = (count - 1) // 2
    giver, taker = tallies[1:1 + 2 * pairs:2], tallies[2:2 + 2 * pairs:2]
    room = jnp.minimum(giver - 1, limit - taker)
    moved = jax.random.randint(jax.random.fold_in(own_key, 1), (pairs,), 0, 1 << 20) % (room + 1)
    tallies = tallies.at[1:1 + 2 * pairs:2].set(giver - moved).at[2:2 + 2 * pairs:2].set(taker + moved)
    return tallies[jax.random.permutation(jax.random.fold_in(own_key, 2), count)]


def normal_values(rng, extent, spread, most, cuts=(), kind=jnp.bfloat16):
    values = spread * jax.random.normal(rng, extent, jnp.float32)
    if cuts:
        values = values * block_scale(rng, extent, cuts, -0.22, 0.18)
    return jnp.clip(values, -most, most).astype(kind)


def setup_inputs(seed: int = 0) -> dict:
    key_of = jax.random.split(jax.random.key(seed), 6)
    return {
        "query": draw_query(jax.random.fold_in(key_of[5], 71), 0),
        "key": draw_key(jax.random.fold_in(key_of[5], 71), 0),
        "value": normal_values(key_of[2], (TOKENS, KVH, HD), 1.0, 6.0, ((0, 512),)),
        "out_grad": normal_values(key_of[3], (TOKENS, HEADS, HD), 1.0, 6.0, ((0, 512),)),
        "doc_lengths": uneven_parts(key_of[4], NDOCS, TOKENS, MOSTDOC, 2).astype(jnp.int32),
    }


def doc_starts(doc_lengths, position):
    ends = jnp.cumsum(doc_lengths)
    begins = ends - doc_lengths
    inside = begins[None, :] <= position[:, None]
    return jnp.max(jnp.where(inside, begins[None, :], 0), axis=1).astype(jnp.int32)


def reference(query, key, value, out_grad, doc_lengths):
    inv_root = HD ** -0.5
    group_size = HEADS // KVH
    window = (REACH + 1) * TOK_DEV
    block_count = TOKENS // TOK_DEV

    def one_block(totals, block_index):
        key_acc, value_acc = totals
        query_first = (block_index * TOK_DEV).astype(jnp.int32)
        key_first = jnp.clip(query_first - REACH * TOK_DEV, 0, TOKENS - window).astype(jnp.int32)
        query_part = lax.dynamic_slice_in_dim(query, query_first, TOK_DEV, 0).astype(jnp.float32)
        query_part = query_part.reshape(TOK_DEV, KVH, group_size, HD)
        grad_part = lax.dynamic_slice_in_dim(out_grad, query_first, TOK_DEV, 0).astype(jnp.float32)
        grad_part = grad_part.reshape(TOK_DEV, KVH, group_size, HD)
        key_part = lax.dynamic_slice_in_dim(key, key_first, window, 0).astype(jnp.float32)
        value_part = lax.dynamic_slice_in_dim(value, key_first, window, 0).astype(jnp.float32)
        query_pos = query_first + jnp.arange(TOK_DEV, dtype=jnp.int32)
        key_pos = key_first + jnp.arange(window, dtype=jnp.int32)
        doc_start = doc_starts(doc_lengths, query_pos)
        allowed = (key_pos[None, :] >= doc_start[:, None]) & (key_pos[None, :] <= query_pos[:, None])
        scores = jnp.einsum("tkgd,skd->kgts", query_part, key_part) * inv_root
        scores = jnp.where(allowed, scores, -1.0e30)
        highest = jnp.max(scores, axis=-1, keepdims=True)
        log_total = highest + jnp.log(jnp.sum(jnp.exp(scores - highest), axis=-1, keepdims=True))
        weights = jnp.where(allowed, jnp.exp(scores - log_total), 0.0).astype(jnp.bfloat16)
        weight_f = weights.astype(jnp.float32)
        attended = jnp.einsum("kgts,skd->tkgd", weight_f, value_part).astype(jnp.bfloat16)
        row_delta = jnp.einsum("tkgd,tkgd->kgt", grad_part, attended.astype(jnp.float32))
        dprob = jnp.einsum("tkgd,skd->kgts", grad_part, value_part)
        dscore = (weight_f * (dprob - row_delta[..., None]) * inv_root).astype(jnp.bfloat16)
        dscore_f = dscore.astype(jnp.float32)
        query_grad = jnp.einsum("kgts,skd->tkgd", dscore_f, key_part).astype(jnp.bfloat16)
        key_term = jnp.einsum("kgts,tkgd->skd", dscore_f, query_part)
        value_term = jnp.einsum("kgts,tkgd->skd", weight_f, grad_part)
        key_old = lax.dynamic_slice_in_dim(key_acc, key_first, window, 0)
        value_old = lax.dynamic_slice_in_dim(value_acc, key_first, window, 0)
        key_acc = lax.dynamic_update_slice_in_dim(key_acc, key_old + key_term, key_first, 0)
        value_acc = lax.dynamic_update_slice_in_dim(value_acc, value_old + value_term, key_first, 0)
        shaped = (attended.reshape(TOK_DEV, HEADS, HD), query_grad.reshape(TOK_DEV, HEADS, HD))
        return (key_acc, value_acc), shaped

    zeros_kv = jnp.zeros((TOKENS, KVH, HD), jnp.float32)
    (key_acc, value_acc), (attended, query_grad) = lax.scan(
        one_block, (zeros_kv, zeros_kv), jnp.arange(block_count, dtype=jnp.int32))
    attended = attended.reshape(TOKENS, HEADS, HD)
    query_grad = query_grad.reshape(TOKENS, HEADS, HD)
    return attended, query_grad, key_acc.astype(jnp.bfloat16), value_acc.astype(jnp.bfloat16)
```

```python
import jax
import jax.numpy as jnp
from jax import lax
from jax.experimental import pallas as pl
from jax.experimental.pallas import tpu as pltpu
from jax.sharding import Mesh, PartitionSpec as P

REACH = 8
NEGATIVE = -1e30
LOG2E = 1.4426950408889634
CORES = 2
QUARTERS = 4
SPANS = REACH // QUARTERS + 1


def dot(a, b, dims):
    return lax.dot_general(a, b, (dims, ((), ())), preferred_element_type=jnp.float32)


def attention_kernel(
    places, lengths, moved, same_core, other_core, out_moved, out_window,
    keys, values, keys_t, values_t, key_sum, value_sum, weight_all, dscore_all,
):
    chunks, _, group, width = moved.shape
    chunk_tok = moved.shape[1] // 2
    rows = chunk_tok * group
    block = chunks * chunk_tok
    span = (REACH + 1) * block
    inv_root = width ** (-0.5)
    scale = inv_root * LOG2E
    z_place, quarter = places[0], places[1]
    window_first = (z_place * QUARTERS + quarter - REACH) * block

    for index in range(REACH + 1):
        place = quarter + index
        near, old = lax.rem(place, QUARTERS), SPANS - 1 - lax.div(place, QUARTERS)
        side = lax.div(near, CORES)
        at_home = lax.rem(near, CORES) == lax.rem(quarter, CORES)
        part = pl.ds(index * block, block)
        key_block = jnp.where(
            at_home, same_core[old, side, :, 0], other_core[old, side, :, 0]
        ).reshape(block, width)
        value_block = jnp.where(
            at_home, same_core[old, side, :, 1], other_core[old, side, :, 1]
        ).reshape(block, width)
        keys[part, :] = key_block
        values[part, :] = value_block
        keys_t[:, part] = key_block.T
        values_t[:, part] = value_block.T

    token = lax.broadcasted_iota(jnp.int32, (1, rows), 1) // group

    def first_keys(chunk):
        position = token + (REACH * block + chunk * chunk_tok) + window_first
        begin = jnp.int32(0)
        start = jnp.zeros((1, rows), jnp.int32)
        for doc in range(lengths.shape[0]):
            start = jnp.where(position >= begin, begin, start)
            begin = begin + lengths[doc]
        return start - window_first

    def part_of(index):
        return pl.ds(index * block, block)

    def lanes_of(chunk):
        return pl.ds(chunk * rows, rows)

    def operands(chunk):
        query = moved[chunk, :chunk_tok].reshape(rows, width)
        grad = moved[chunk, chunk_tok:].reshape(rows, width)
        return query, grad

    def live(index, chunk):
        low = chunk * chunk_tok if index == 0 else 0
        high = (chunk + 1) * chunk_tok if index == REACH else block
        return low, high

    def rows_of(index, chunk):
        low, high = live(index, chunk)
        return pl.ds(index * block + low, high - low)

    def clear(held, chunk):
        before, after = chunk * chunk_tok, block - (chunk + 1) * chunk_tok
        if before:
            held[pl.ds(0, before), lanes_of(chunk)] = jnp.zeros((before, rows), held.dtype)
        if after:
            held[pl.ds(span - after, after), lanes_of(chunk)] = jnp.zeros((after, rows), held.dtype)

    state = {}

    def forward(chunk):
        query, _ = operands(chunk)
        low = first_keys(chunk)
        highest, total, seen = None, None, {}
        for index in [REACH] + list(range(REACH)):
            scores = dot(keys[rows_of(index, chunk), :], query, ((1,), (1,)))
            first, last = live(index, chunk)
            key_row = lax.broadcasted_iota(jnp.int32, (last - first, rows), 0) + first
            allowed = key_row >= low - index * block
            if index == REACH:
                allowed = allowed & (key_row <= token + chunk * chunk_tok)
            scores = jnp.where(allowed, scores, NEGATIVE)
            most = jnp.max(scores, axis=0, keepdims=True)
            if highest is None:
                weights = jnp.exp2((scores - most) * scale)
                total = jnp.sum(weights, axis=0, keepdims=True)
            else:
                most = jnp.maximum(most, highest)
                weights = jnp.exp2((scores - most) * scale)
                total = total * jnp.exp2((highest - most) * scale)
                total = total + jnp.sum(weights, axis=0, keepdims=True)
            highest = most
            seen[index] = most
            weight_all[rows_of(index, chunk), lanes_of(chunk)] = weights.astype(jnp.bfloat16)
            yield
        clear(weight_all, chunk)
        inverse = 1.0 / total
        state[chunk] = {
            index: jnp.exp2((most - highest) * scale) * inverse for index, most in seen.items()
        }

    def backward(chunk):
        query, grad = operands(chunk)
        factors = state.pop(chunk)
        for index in range(REACH + 1):
            part = rows_of(index, chunk)
            weights = weight_all[part, lanes_of(chunk)].astype(jnp.float32)
            weight_all[part, lanes_of(chunk)] = (weights * factors[index]).astype(jnp.bfloat16)
            if index % 3 == 2:
                yield
        attended = dot(values_t[...], weight_all[:, lanes_of(chunk)], ((1,), (0,)))
        attended = attended.astype(jnp.bfloat16)
        out_moved[chunk, :chunk_tok] = attended.T.reshape(chunk_tok, group, width)
        delta = jnp.sum(
            grad.T.astype(jnp.float32) * attended.astype(jnp.float32), axis=0, keepdims=True
        )
        yield
        for index in range(REACH + 1):
            part = rows_of(index, chunk)
            dprob = dot(values[part, :], grad, ((1,), (1,)))
            weights = weight_all[part, lanes_of(chunk)].astype(jnp.float32)
            dscore_all[part, lanes_of(chunk)] = (weights * (dprob - delta)).astype(jnp.bfloat16)
            yield
        clear(dscore_all, chunk)
        query_grad = dot(keys_t[...], dscore_all[:, lanes_of(chunk)], ((1,), (0,))) * inv_root
        query_grad = query_grad.astype(jnp.bfloat16)
        out_moved[chunk, chunk_tok : 2 * chunk_tok] = query_grad.T.reshape(chunk_tok, group, width)
        yield

    def gather(first, count):
        lanes = pl.ds(first * rows, count * rows)
        chosen = pl.ds(first, count)
        query = moved[chosen, :chunk_tok].reshape(count * rows, width)
        grad = moved[chosen, chunk_tok:].reshape(count * rows, width)
        for index in range(REACH + 1):
            part = part_of(index)
            value_part = dot(weight_all[part, lanes], grad, ((1,), (0,)))
            key_part = dot(dscore_all[part, lanes], query, ((1,), (0,)))
            if first:
                value_part = value_part + value_sum[part, :]
                key_part = key_part + key_sum[part, :]
            value_sum[part, :] = value_part
            key_sum[part, :] = key_part
            if index % 3 == 2:
                yield

    def together(*streams):
        streams = list(streams)
        while streams:
            for stream in list(streams):
                if next(stream, streams) is streams:
                    streams.remove(stream)

    together(forward(0))
    for chunk in range(chunks):
        streams = [backward(chunk)]
        if chunk + 1 < chunks:
            streams.append(forward(chunk + 1))
        if chunk and chunk % 2 == 0:
            streams.append(gather(chunk - 2, 2))
        if chunk == chunks - 1:
            streams.append(gather(chunk - 1, 1))
        together(*streams)
    together(gather(chunks - 1, 1))

    shape = (chunks, chunk_tok, width)
    blank = jnp.zeros((chunks, 2, chunk_tok, width), out_window.dtype)
    for index in range(QUARTERS * SPANS):
        place = lax.rem(quarter + index, QUARTERS * SPANS)
        near, plane = lax.rem(place, QUARTERS), lax.div(place, QUARTERS)
        away = lax.rem(near + quarter, CORES)
        side = lax.div(near, CORES)
        if index <= REACH:
            part = part_of(index)
            out_window[away, plane, side, :, 0] = (key_sum[part, :] * inv_root).reshape(shape)
            out_window[away, plane, side, :, 1] = value_sum[part, :].reshape(shape)
        else:
            out_window[away, plane, side] = blank


def attention(places, lengths, moved, same_core, other_core):
    chunks, twice, group, width = moved.shape
    chunk_tok = twice // 2
    block = chunks * chunk_tok
    span = (REACH + 1) * block
    vmem = pl.BlockSpec(memory_space=pltpu.VMEM)
    smem = pl.BlockSpec(memory_space=pltpu.SMEM)
    return pl.pallas_call(
        attention_kernel,
        out_shape=(
            jax.ShapeDtypeStruct(moved.shape, jnp.bfloat16),
            jax.ShapeDtypeStruct((CORES,) + same_core.shape, jnp.float32),
        ),
        in_specs=[smem, smem, vmem, vmem, vmem],
        out_specs=(vmem, vmem),
        scratch_shapes=[
            pltpu.VMEM((span, width), jnp.bfloat16),
            pltpu.VMEM((span, width), jnp.bfloat16),
            pltpu.VMEM((width, span), jnp.bfloat16),
            pltpu.VMEM((width, span), jnp.bfloat16),
            pltpu.VMEM((span, width), jnp.float32),
            pltpu.VMEM((span, width), jnp.float32),
            pltpu.VMEM((span, block * group), jnp.bfloat16),
            pltpu.VMEM((span, block * group), jnp.bfloat16),
        ],
        compiler_params=pltpu.CompilerParams(vmem_limit_bytes=40 * 1024 * 1024),
        cost_estimate=pl.CostEstimate(
            flops=12 * block * group * span * width,
            bytes_accessed=4 * moved.size + 4 * same_core.size,
            transcendentals=block * group * span,
        ),
        name="attention",
    )(places, lengths, moved, same_core, other_core)


def spread_kernel(back, attended, query_grad, sems):
    kv_heads, _, group, _ = back.shape
    tokens = attended.shape[0]
    copies = []
    for index in range(kv_heads):
        heads = pl.ds(index * group, group)
        for which, target in enumerate((attended, query_grad)):
            copies.append(
                pltpu.make_async_copy(
                    back.at[index, pl.ds(which * tokens, tokens)],
                    target.at[:, heads, :],
                    sems.at[2 * index + which],
                )
            )
            copies[-1].start()
    for copy in copies:
        copy.wait()


def spread(back, query):
    anywhere = pl.BlockSpec(memory_space=pl.ANY)
    large = jax.ShapeDtypeStruct(query.shape, jnp.bfloat16)
    return pl.pallas_call(
        spread_kernel,
        out_shape=(large, large),
        in_specs=[pl.BlockSpec(memory_space=pltpu.VMEM)],
        out_specs=(anywhere, anywhere),
        scratch_shapes=[pltpu.SemaphoreType.DMA((2 * back.shape[0],))],
        compiler_params=pltpu.CompilerParams(vmem_limit_bytes=16 * 1024 * 1024),
        name="spread",
    )(back)


def split_kernel(total, key_grad, value_grad, spread):
    for which, target in enumerate((key_grad, value_grad)):
        for index in range(total.shape[1]):
            both = total[0, index, which].astype(jnp.float32)
            spread[:, index, :] = both + total[1, index, which].astype(jnp.float32)
        target[...] = spread[...].astype(jnp.bfloat16)


def split(total, key):
    vmem = pl.BlockSpec(memory_space=pltpu.VMEM)
    small = jax.ShapeDtypeStruct(key.shape, jnp.bfloat16)
    return pl.pallas_call(
        split_kernel,
        out_shape=(small, small),
        in_specs=[vmem],
        out_specs=(vmem, vmem),
        scratch_shapes=[pltpu.VMEM(key.shape, jnp.float32)],
        compiler_params=pltpu.CompilerParams(vmem_limit_bytes=16 * 1024 * 1024),
        name="split",
    )(total)


def turned(block, axis, distance):
    size = lax.axis_size(axis)
    return lax.ppermute(block, axis, [(i, (i + distance) % size) for i in range(size)])


def swapped(block):
    return lax.all_to_all(block, "head", split_axis=0, concat_axis=0, tiled=True)


def crossed(block):
    flat = block.reshape((-1,) + block.shape[2:])
    flat = lax.all_to_all(flat, ("yhi", "head"), split_axis=0, concat_axis=0, tiled=True)
    return flat.reshape(block.shape)


def on_device(query, key, value, out_grad, doc_lengths):
    tokens, heads, width = query.shape
    kv_heads = key.shape[1]
    group = heads // kv_heads

    pair = jnp.transpose(jnp.stack([key, value]), (2, 0, 1, 3))
    pair = crossed(jnp.broadcast_to(pair[None], (QUARTERS // CORES,) + pair.shape))
    both = jnp.stack([query, out_grad]).reshape(2 * tokens, kv_heads, group, width)
    both = jnp.transpose(both, (1, 0, 2, 3))
    pair, both = lax.optimization_barrier((pair, both))
    moved = swapped(both)
    layers = [pair] + [turned(pair, "z", distance) for distance in range(1, SPANS)]
    same_core = jnp.stack(layers)
    other_core = turned(same_core, "core", 1)

    quarter = lax.axis_index("yhi") * CORES + lax.axis_index("core")
    places = jnp.stack([lax.axis_index("z"), quarter]).astype(jnp.int32)
    out_moved, out_window = attention(places, doc_lengths, moved, same_core, other_core)

    back = swapped(out_moved)
    beside = turned(out_window[1].astype(jnp.bfloat16), "core", 1)
    own = out_window[0] + beside.astype(jnp.float32)
    total = own[SPANS - 1]
    for distance in range(1, SPANS):
        sent = turned(own[SPANS - 1 - distance].astype(jnp.bfloat16), "z", -distance)
        total = total + sent.astype(jnp.float32)
    back, total = lax.optimization_barrier((back, total.astype(jnp.bfloat16)))
    total = crossed(total)
    attended, query_grad = spread(back, query)
    key_grad, value_grad = split(total, key)
    return attended, query_grad, key_grad, value_grad


def solution(mesh):
    ctx, head = mesh.devices.shape
    finer = Mesh(
        mesh.devices.reshape(ctx // QUARTERS, QUARTERS // CORES, CORES, head),
        ("z", "yhi", "core", "head"),
    )
    token_split = P(("z", "yhi", "core", "head"), None, None)
    return jax.shard_map(
        on_device,
        mesh=finer,
        in_specs=(token_split,) * 4 + (P(),),
        out_specs=(token_split,) * 4,
        check_vma=False,
    )
```

```python
import jax
import jax.numpy as jnp
from jax import lax
from jax.experimental import pallas as pl
from jax.experimental.pallas import tpu as pltpu
from jax.sharding import Mesh, PartitionSpec as P

REACH = 8
NEGATIVE = -1e30
LOG2E = 1.4426950408889634
CORES = 2
QUARTERS = 4
SPANS = REACH // QUARTERS + 1


def dot(a, b, dims):
    return lax.dot_general(a, b, (dims, ((), ())), preferred_element_type=jnp.float32)


def attention_kernel(
    places, lengths, moved, same_core, other_core, out_moved, out_window,
    keys, values, keys_t, values_t, key_sum, value_sum, weight_all, dscore_all,
):
    chunks, _, group, width = moved.shape
    chunk_tok = moved.shape[1] // 2
    rows = chunk_tok * group
    block = chunks * chunk_tok
    span = (REACH + 1) * block
    inv_root = width ** (-0.5)
    scale = inv_root * LOG2E
    z_place, quarter = places[0], places[1]
    window_first = (z_place * QUARTERS + quarter - REACH) * block

    for index in range(REACH + 1):
        place = quarter + index
        near, old = lax.rem(place, QUARTERS), SPANS - 1 - lax.div(place, QUARTERS)
        side = lax.div(near, CORES)
        at_home = lax.rem(near, CORES) == lax.rem(quarter, CORES)
        part = pl.ds(index * block, block)
        key_block = jnp.where(
            at_home, same_core[old, side, :, 0], other_core[old, side, :, 0]
        ).reshape(block, width)
        value_block = jnp.where(
            at_home, same_core[old, side, :, 1], other_core[old, side, :, 1]
        ).reshape(block, width)
        keys[part, :] = key_block
        values[part, :] = value_block
        keys_t[:, part] = key_block.T
        values_t[:, part] = value_block.T

    token = lax.broadcasted_iota(jnp.int32, (1, rows), 1) // group

    def first_keys(chunk):
        position = token + (REACH * block + chunk * chunk_tok) + window_first
        begin = jnp.int32(0)
        start = jnp.zeros((1, rows), jnp.int32)
        for doc in range(lengths.shape[0]):
            start = jnp.where(position >= begin, begin, start)
            begin = begin + lengths[doc]
        return start - window_first

    def part_of(index):
        return pl.ds(index * block, block)

    def lanes_of(chunk):
        return pl.ds(chunk * rows, rows)

    def operands(chunk):
        query = moved[chunk, :chunk_tok].reshape(rows, width)
        grad = moved[chunk, chunk_tok:].reshape(rows, width)
        return query, grad

    def live(index, chunk):
        low = chunk * chunk_tok if index == 0 else 0
        high = (chunk + 1) * chunk_tok if index == REACH else block
        return low, high

    def rows_of(index, chunk):
        low, high = live(index, chunk)
        return pl.ds(index * block + low, high - low)

    def clear(held, chunk):
        before, after = chunk * chunk_tok, block - (chunk + 1) * chunk_tok
        if before:
            held[pl.ds(0, before), lanes_of(chunk)] = jnp.zeros((before, rows), held.dtype)
        if after:
            held[pl.ds(span - after, after), lanes_of(chunk)] = jnp.zeros((after, rows), held.dtype)

    state = {}

    def forward(chunk):
        query, _ = operands(chunk)
        low = first_keys(chunk)
        highest, total, seen = None, None, {}
        for index in [REACH] + list(range(REACH)):
            scores = dot(keys[rows_of(index, chunk), :], query, ((1,), (1,)))
            first, last = live(index, chunk)
            key_row = lax.broadcasted_iota(jnp.int32, (last - first, rows), 0) + first
            allowed = key_row >= low - index * block
            if index == REACH:
                allowed = allowed & (key_row <= token + chunk * chunk_tok)
            scores = jnp.where(allowed, scores, NEGATIVE)
            most = jnp.max(scores, axis=0, keepdims=True)
            if highest is None:
                weights = jnp.exp2((scores - most) * scale)
                total = jnp.sum(weights, axis=0, keepdims=True)
            else:
                most = jnp.maximum(most, highest)
                weights = jnp.exp2((scores - most) * scale)
                total = total * jnp.exp2((highest - most) * scale)
                total = total + jnp.sum(weights, axis=0, keepdims=True)
            highest = most
            seen[index] = most
            weight_all[rows_of(index, chunk), lanes_of(chunk)] = weights.astype(jnp.bfloat16)
            yield
        clear(weight_all, chunk)
        inverse = 1.0 / total
        state[chunk] = {
            index: (jnp.exp2((most - highest) * scale) * inverse).astype(jnp.bfloat16)
            for index, most in seen.items()
        }

    def backward(chunk):
        query, grad = operands(chunk)
        factors = state.pop(chunk)
        for index in range(REACH + 1):
            part = rows_of(index, chunk)
            weight_all[part, lanes_of(chunk)] = weight_all[part, lanes_of(chunk)] * factors[index]
            if index % 3 == 2:
                yield
        attended = dot(values_t[...], weight_all[:, lanes_of(chunk)], ((1,), (0,)))
        attended = attended.astype(jnp.bfloat16)
        out_moved[chunk, :chunk_tok] = attended.T.reshape(chunk_tok, group, width)
        delta = jnp.sum(
            grad.T.astype(jnp.float32) * attended.astype(jnp.float32), axis=0, keepdims=True
        )
        yield
        for index in range(REACH + 1):
            part = rows_of(index, chunk)
            dprob = dot(values[part, :], grad, ((1,), (1,)))
            slope = (dprob - delta).astype(jnp.bfloat16)
            dscore_all[part, lanes_of(chunk)] = weight_all[part, lanes_of(chunk)] * slope
            yield
        clear(dscore_all, chunk)
        query_grad = dot(keys_t[...], dscore_all[:, lanes_of(chunk)], ((1,), (0,))) * inv_root
        query_grad = query_grad.astype(jnp.bfloat16)
        out_moved[chunk, chunk_tok : 2 * chunk_tok] = query_grad.T.reshape(chunk_tok, group, width)
        yield

    def gather(first, count):
        lanes = pl.ds(first * rows, count * rows)
        chosen = pl.ds(first, count)
        query = moved[chosen, :chunk_tok].reshape(count * rows, width)
        grad = moved[chosen, chunk_tok:].reshape(count * rows, width)
        for index in range(REACH + 1):
            part = part_of(index)
            value_part = dot(weight_all[part, lanes], grad, ((1,), (0,)))
            key_part = dot(dscore_all[part, lanes], query, ((1,), (0,)))
            if first:
                value_part = value_part + value_sum[part, :]
                key_part = key_part + key_sum[part, :]
            value_sum[part, :] = value_part
            key_sum[part, :] = key_part
            if index % 3 == 2:
                yield

    def together(*streams):
        streams = list(streams)
        while streams:
            for stream in list(streams):
                if next(stream, streams) is streams:
                    streams.remove(stream)

    together(forward(0))
    for chunk in range(chunks):
        streams = [backward(chunk)]
        if chunk + 1 < chunks:
            streams.append(forward(chunk + 1))
        if chunk and chunk % 2 == 0:
            streams.append(gather(chunk - 2, 2))
        if chunk == chunks - 1:
            streams.append(gather(chunk - 1, 1))
        together(*streams)
    together(gather(chunks - 1, 1))

    shape = (chunks, chunk_tok, width)
    blank = jnp.zeros((chunks, 2, chunk_tok, width), out_window.dtype)
    for index in range(QUARTERS * SPANS):
        place = lax.rem(quarter + index, QUARTERS * SPANS)
        near, plane = lax.rem(place, QUARTERS), lax.div(place, QUARTERS)
        away = lax.rem(near + quarter, CORES)
        side = lax.div(near, CORES)
        if index <= REACH:
            part = part_of(index)
            out_window[away, plane, side, :, 0] = (key_sum[part, :] * inv_root).reshape(shape)
            out_window[away, plane, side, :, 1] = value_sum[part, :].reshape(shape)
        else:
            out_window[away, plane, side] = blank


def attention(places, lengths, moved, same_core, other_core):
    chunks, twice, group, width = moved.shape
    chunk_tok = twice // 2
    block = chunks * chunk_tok
    span = (REACH + 1) * block
    vmem = pl.BlockSpec(memory_space=pltpu.VMEM)
    smem = pl.BlockSpec(memory_space=pltpu.SMEM)
    return pl.pallas_call(
        attention_kernel,
        out_shape=(
            jax.ShapeDtypeStruct(moved.shape, jnp.bfloat16),
            jax.ShapeDtypeStruct((CORES,) + same_core.shape, jnp.float32),
        ),
        in_specs=[smem, smem, vmem, vmem, vmem],
        out_specs=(vmem, vmem),
        scratch_shapes=[
            pltpu.VMEM((span, width), jnp.bfloat16),
            pltpu.VMEM((span, width), jnp.bfloat16),
            pltpu.VMEM((width, span), jnp.bfloat16),
            pltpu.VMEM((width, span), jnp.bfloat16),
            pltpu.VMEM((span, width), jnp.float32),
            pltpu.VMEM((span, width), jnp.float32),
            pltpu.VMEM((span, block * group), jnp.bfloat16),
            pltpu.VMEM((span, block * group), jnp.bfloat16),
        ],
        compiler_params=pltpu.CompilerParams(vmem_limit_bytes=40 * 1024 * 1024),
        cost_estimate=pl.CostEstimate(
            flops=12 * block * group * span * width,
            bytes_accessed=4 * moved.size + 4 * same_core.size,
            transcendentals=block * group * span,
        ),
        name="attention",
    )(places, lengths, moved, same_core, other_core)


def spread_kernel(back, attended, query_grad, sems):
    kv_heads, _, group, _ = back.shape
    tokens = attended.shape[0]
    copies = []
    for index in range(kv_heads):
        heads = pl.ds(index * group, group)
        for which, target in enumerate((attended, query_grad)):
            copies.append(
                pltpu.make_async_copy(
                    back.at[index, pl.ds(which * tokens, tokens)],
                    target.at[:, heads, :],
                    sems.at[2 * index + which],
                )
            )
            copies[-1].start()
    for copy in copies:
        copy.wait()


def spread(back, query):
    anywhere = pl.BlockSpec(memory_space=pl.ANY)
    large = jax.ShapeDtypeStruct(query.shape, jnp.bfloat16)
    return pl.pallas_call(
        spread_kernel,
        out_shape=(large, large),
        in_specs=[pl.BlockSpec(memory_space=pltpu.VMEM)],
        out_specs=(anywhere, anywhere),
        scratch_shapes=[pltpu.SemaphoreType.DMA((2 * back.shape[0],))],
        compiler_params=pltpu.CompilerParams(vmem_limit_bytes=16 * 1024 * 1024),
        name="spread",
    )(back)


def split_kernel(total, key_grad, value_grad, spread):
    for which, target in enumerate((key_grad, value_grad)):
        for index in range(total.shape[1]):
            both = total[0, index, which].astype(jnp.float32)
            spread[:, index, :] = both + total[1, index, which].astype(jnp.float32)
        target[...] = spread[...].astype(jnp.bfloat16)


def split(total, key):
    vmem = pl.BlockSpec(memory_space=pltpu.VMEM)
    small = jax.ShapeDtypeStruct(key.shape, jnp.bfloat16)
    return pl.pallas_call(
        split_kernel,
        out_shape=(small, small),
        in_specs=[vmem],
        out_specs=(vmem, vmem),
        scratch_shapes=[pltpu.VMEM(key.shape, jnp.float32)],
        compiler_params=pltpu.CompilerParams(vmem_limit_bytes=16 * 1024 * 1024),
        name="split",
    )(total)


def turned(block, axis, distance):
    size = lax.axis_size(axis)
    return lax.ppermute(block, axis, [(i, (i + distance) % size) for i in range(size)])


def swapped(block):
    return lax.all_to_all(block, "head", split_axis=0, concat_axis=0, tiled=True)


def crossed(block):
    flat = block.reshape((-1,) + block.shape[2:])
    flat = lax.all_to_all(flat, ("yhi", "head"), split_axis=0, concat_axis=0, tiled=True)
    return flat.reshape(block.shape)


def on_device(query, key, value, out_grad, doc_lengths):
    tokens, heads, width = query.shape
    kv_heads = key.shape[1]
    group = heads // kv_heads

    pair = jnp.transpose(jnp.stack([key, value]), (2, 0, 1, 3))
    pair = crossed(jnp.broadcast_to(pair[None], (QUARTERS // CORES,) + pair.shape))
    both = jnp.stack([query, out_grad]).reshape(2 * tokens, kv_heads, group, width)
    both = jnp.transpose(both, (1, 0, 2, 3))
    pair, both = lax.optimization_barrier((pair, both))
    moved = swapped(both)
    layers = [pair] + [turned(pair, "z", distance) for distance in range(1, SPANS)]
    same_core = jnp.stack(layers)
    other_core = turned(same_core, "core", 1)

    quarter = lax.axis_index("yhi") * CORES + lax.axis_index("core")
    places = jnp.stack([lax.axis_index("z"), quarter]).astype(jnp.int32)
    out_moved, out_window = attention(places, doc_lengths, moved, same_core, other_core)

    back = swapped(out_moved)
    beside = turned(out_window[1].astype(jnp.bfloat16), "core", 1)
    own = out_window[0] + beside.astype(jnp.float32)
    total = own[SPANS - 1]
    for distance in range(1, SPANS):
        sent = turned(own[SPANS - 1 - distance].astype(jnp.bfloat16), "z", -distance)
        total = total + sent.astype(jnp.float32)
    back, total = lax.optimization_barrier((back, total.astype(jnp.bfloat16)))
    total = crossed(total)
    attended, query_grad = spread(back, query)
    key_grad, value_grad = split(total, key)
    return attended, query_grad, key_grad, value_grad


def solution(mesh):
    ctx, head = mesh.devices.shape
    finer = Mesh(
        mesh.devices.reshape(ctx // QUARTERS, QUARTERS // CORES, CORES, head),
        ("z", "yhi", "core", "head"),
    )
    token_split = P(("z", "yhi", "core", "head"), None, None)
    return jax.shard_map(
        on_device,
        mesh=finer,
        in_specs=(token_split,) * 4 + (P(),),
        out_specs=(token_split,) * 4,
        check_vma=False,
    )
```

```python
import jax
import jax.numpy as jnp
from jax import lax
from jax.experimental import pallas as pl
from jax.experimental.pallas import tpu as pltpu
from jax.sharding import Mesh, PartitionSpec as P

REACH = 8
NEGATIVE = -1e30
LOG2E = 1.4426950408889634
CORES = 2
QUARTERS = 4
SPANS = REACH // QUARTERS + 1


def dot(a, b, dims):
    return lax.dot_general(a, b, (dims, ((), ())), preferred_element_type=jnp.float32)


def attention_kernel(
    places, lengths, moved, same_core, other_core, out_moved, out_window,
    keys, values, keys_t, values_t, key_sum, value_sum, weight_all, dscore_all, ready, sems,
):
    chunks, _, group, width = moved.shape
    chunk_tok = moved.shape[1] // 2
    rows = chunk_tok * group
    block = chunks * chunk_tok
    span = (REACH + 1) * block
    inv_root = width ** (-0.5)
    scale = inv_root * LOG2E
    z_place, quarter = places[0], places[1]
    window_first = (z_place * QUARTERS + quarter - REACH) * block

    for index in range(REACH + 1):
        place = quarter + index
        near, old = lax.rem(place, QUARTERS), SPANS - 1 - lax.div(place, QUARTERS)
        side = lax.div(near, CORES)
        at_home = lax.rem(near, CORES) == lax.rem(quarter, CORES)
        part = pl.ds(index * block, block)
        key_block = jnp.where(
            at_home, same_core[old, side, :, 0], other_core[old, side, :, 0]
        ).reshape(block, width)
        value_block = jnp.where(
            at_home, same_core[old, side, :, 1], other_core[old, side, :, 1]
        ).reshape(block, width)
        keys[part, :] = key_block
        values[part, :] = value_block
        keys_t[:, part] = key_block.T
        values_t[:, part] = value_block.T

    token = lax.broadcasted_iota(jnp.int32, (1, rows), 1) // group

    def first_keys(chunk):
        position = token + (REACH * block + chunk * chunk_tok) + window_first
        begin = jnp.int32(0)
        start = jnp.zeros((1, rows), jnp.int32)
        for doc in range(lengths.shape[0]):
            start = jnp.where(position >= begin, begin, start)
            begin = begin + lengths[doc]
        return start - window_first

    def part_of(index):
        return pl.ds(index * block, block)

    def lanes_of(chunk):
        return pl.ds(chunk * rows, rows)

    def operands(chunk):
        query = moved[chunk, :chunk_tok].reshape(rows, width)
        grad = moved[chunk, chunk_tok:].reshape(rows, width)
        return query, grad

    def live(index, chunk):
        low = chunk * chunk_tok if index == 0 else 0
        high = (chunk + 1) * chunk_tok if index == REACH else block
        return low, high

    def rows_of(index, chunk):
        low, high = live(index, chunk)
        return pl.ds(index * block + low, high - low)

    def clear(held, chunk):
        before, after = chunk * chunk_tok, block - (chunk + 1) * chunk_tok
        if before:
            held[pl.ds(0, before), lanes_of(chunk)] = jnp.zeros((before, rows), held.dtype)
        if after:
            held[pl.ds(span - after, after), lanes_of(chunk)] = jnp.zeros((after, rows), held.dtype)

    state = {}

    def leaving(chunk):
        return pltpu.make_async_copy(ready.at[chunk], out_moved.at[chunk], sems.at[chunk])

    def forward(chunk):
        query, _ = operands(chunk)
        low = first_keys(chunk)
        highest, total, seen = None, None, {}
        for index in [REACH] + list(range(REACH)):
            scores = dot(keys[rows_of(index, chunk), :], query, ((1,), (1,)))
            first, last = live(index, chunk)
            key_row = lax.broadcasted_iota(jnp.int32, (last - first, rows), 0) + first
            allowed = key_row >= low - index * block
            if index == REACH:
                allowed = allowed & (key_row <= token + chunk * chunk_tok)
            scores = jnp.where(allowed, scores, NEGATIVE)
            most = jnp.max(scores, axis=0, keepdims=True)
            if highest is None:
                weights = jnp.exp2((scores - most) * scale)
                total = jnp.sum(weights, axis=0, keepdims=True)
            else:
                most = jnp.maximum(most, highest)
                weights = jnp.exp2((scores - most) * scale)
                total = total * jnp.exp2((highest - most) * scale)
                total = total + jnp.sum(weights, axis=0, keepdims=True)
            highest = most
            seen[index] = most
            weight_all[rows_of(index, chunk), lanes_of(chunk)] = weights.astype(jnp.bfloat16)
            yield
        clear(weight_all, chunk)
        inverse = 1.0 / total
        state[chunk] = {
            index: (jnp.exp2((most - highest) * scale) * inverse).astype(jnp.bfloat16)
            for index, most in seen.items()
        }

    def backward(chunk):
        query, grad = operands(chunk)
        factors = state.pop(chunk)
        for index in range(REACH + 1):
            part = rows_of(index, chunk)
            weight_all[part, lanes_of(chunk)] = weight_all[part, lanes_of(chunk)] * factors[index]
            if index % 3 == 2:
                yield
        attended = dot(values_t[...], weight_all[:, lanes_of(chunk)], ((1,), (0,)))
        attended = attended.astype(jnp.bfloat16)
        ready[chunk, :chunk_tok] = attended.T.reshape(chunk_tok, group, width)
        delta = jnp.sum(
            grad.T.astype(jnp.float32) * attended.astype(jnp.float32), axis=0, keepdims=True
        )
        yield
        for index in range(REACH + 1):
            part = rows_of(index, chunk)
            dprob = dot(values[part, :], grad, ((1,), (1,)))
            slope = (dprob - delta).astype(jnp.bfloat16)
            dscore_all[part, lanes_of(chunk)] = weight_all[part, lanes_of(chunk)] * slope
            yield
        clear(dscore_all, chunk)
        query_grad = dot(keys_t[...], dscore_all[:, lanes_of(chunk)], ((1,), (0,))) * inv_root
        query_grad = query_grad.astype(jnp.bfloat16)
        ready[chunk, chunk_tok:] = query_grad.T.reshape(chunk_tok, group, width)
        leaving(chunk).start()
        yield

    def gather(first, count):
        lanes = pl.ds(first * rows, count * rows)
        chosen = pl.ds(first, count)
        query = moved[chosen, :chunk_tok].reshape(count * rows, width)
        grad = moved[chosen, chunk_tok:].reshape(count * rows, width)
        for index in range(REACH + 1):
            low, high = index * block, (index + 1) * block
            if index == 0:
                low = first * chunk_tok
            if index == REACH:
                high = low + (first + count) * chunk_tok
                if not first:
                    rest = pl.ds(high, span - high)
                    value_sum[rest, :] = jnp.zeros((span - high, width), jnp.float32)
                    key_sum[rest, :] = jnp.zeros((span - high, width), jnp.float32)
            part = pl.ds(low, high - low)
            value_part = dot(weight_all[part, lanes], grad, ((1,), (0,)))
            key_part = dot(dscore_all[part, lanes], query, ((1,), (0,)))
            if first:
                value_part = value_part + value_sum[part, :]
                key_part = key_part + key_sum[part, :]
            value_sum[part, :] = value_part
            key_sum[part, :] = key_part
            if index % 3 == 2:
                yield

    def together(*streams):
        streams = list(streams)
        while streams:
            for stream in list(streams):
                if next(stream, streams) is streams:
                    streams.remove(stream)

    together(forward(0))
    for chunk in range(chunks):
        streams = [backward(chunk)]
        if chunk + 1 < chunks:
            streams.append(forward(chunk + 1))
        if chunk and chunk % 2 == 0:
            streams.append(gather(chunk - 2, 2))
        if chunk == chunks - 1:
            streams.append(gather(chunk - 1, 1))
        together(*streams)
    together(gather(chunks - 1, 1))

    shape = (chunks, chunk_tok, width)
    blank = jnp.zeros((chunks, 2, chunk_tok, width), out_window.dtype)
    for index in range(QUARTERS * SPANS):
        place = lax.rem(quarter + index, QUARTERS * SPANS)
        near, plane = lax.rem(place, QUARTERS), lax.div(place, QUARTERS)
        away = lax.rem(near + quarter, CORES)
        side = lax.div(near, CORES)
        if index <= REACH:
            part = part_of(index)
            out_window[away, plane, side, :, 0] = (key_sum[part, :] * inv_root).reshape(shape)
            out_window[away, plane, side, :, 1] = value_sum[part, :].reshape(shape)
        else:
            out_window[away, plane, side] = blank
    for chunk in range(chunks):
        leaving(chunk).wait()


def attention(places, lengths, moved, same_core, other_core):
    chunks, twice, group, width = moved.shape
    chunk_tok = twice // 2
    block = chunks * chunk_tok
    span = (REACH + 1) * block
    vmem = pl.BlockSpec(memory_space=pltpu.VMEM)
    smem = pl.BlockSpec(memory_space=pltpu.SMEM)
    return pl.pallas_call(
        attention_kernel,
        out_shape=(
            jax.ShapeDtypeStruct(moved.shape, jnp.bfloat16),
            jax.ShapeDtypeStruct((CORES,) + same_core.shape, jnp.float32),
        ),
        in_specs=[smem, smem, vmem, vmem, vmem],
        out_specs=(pl.BlockSpec(memory_space=pl.ANY), vmem),
        scratch_shapes=[
            pltpu.VMEM((span, width), jnp.bfloat16),
            pltpu.VMEM((span, width), jnp.bfloat16),
            pltpu.VMEM((width, span), jnp.bfloat16),
            pltpu.VMEM((width, span), jnp.bfloat16),
            pltpu.VMEM((span, width), jnp.float32),
            pltpu.VMEM((span, width), jnp.float32),
            pltpu.VMEM((span, block * group), jnp.bfloat16),
            pltpu.VMEM((span, block * group), jnp.bfloat16),
            pltpu.VMEM(moved.shape, jnp.bfloat16),
            pltpu.SemaphoreType.DMA((chunks,)),
        ],
        compiler_params=pltpu.CompilerParams(vmem_limit_bytes=40 * 1024 * 1024),
        cost_estimate=pl.CostEstimate(
            flops=12 * block * group * span * width,
            bytes_accessed=4 * moved.size + 4 * same_core.size,
            transcendentals=block * group * span,
        ),
        name="attention",
    )(places, lengths, moved, same_core, other_core)


def spread_kernel(back, attended, query_grad, sems):
    kv_heads, _, group, _ = back.shape
    tokens = attended.shape[0]
    copies = []
    for index in range(kv_heads):
        heads = pl.ds(index * group, group)
        for which, target in enumerate((attended, query_grad)):
            copies.append(
                pltpu.make_async_copy(
                    back.at[index, pl.ds(which * tokens, tokens)],
                    target.at[:, heads, :],
                    sems.at[2 * index + which],
                )
            )
            copies[-1].start()
    for copy in copies:
        copy.wait()


def spread(back, query):
    anywhere = pl.BlockSpec(memory_space=pl.ANY)
    large = jax.ShapeDtypeStruct(query.shape, jnp.bfloat16)
    return pl.pallas_call(
        spread_kernel,
        out_shape=(large, large),
        in_specs=[pl.BlockSpec(memory_space=pltpu.VMEM)],
        out_specs=(anywhere, anywhere),
        scratch_shapes=[pltpu.SemaphoreType.DMA((2 * back.shape[0],))],
        compiler_params=pltpu.CompilerParams(vmem_limit_bytes=16 * 1024 * 1024),
        name="spread",
    )(back)


def split_kernel(total, key_grad, value_grad, spread):
    for which, target in enumerate((key_grad, value_grad)):
        for index in range(total.shape[1]):
            both = total[0, index, which].astype(jnp.float32)
            spread[:, index, :] = both + total[1, index, which].astype(jnp.float32)
        target[...] = spread[...].astype(jnp.bfloat16)


def split(total, key):
    vmem = pl.BlockSpec(memory_space=pltpu.VMEM)
    small = jax.ShapeDtypeStruct(key.shape, jnp.bfloat16)
    return pl.pallas_call(
        split_kernel,
        out_shape=(small, small),
        in_specs=[vmem],
        out_specs=(vmem, vmem),
        scratch_shapes=[pltpu.VMEM(key.shape, jnp.float32)],
        compiler_params=pltpu.CompilerParams(vmem_limit_bytes=16 * 1024 * 1024),
        name="split",
    )(total)


def turned(block, axis, distance):
    size = lax.axis_size(axis)
    return lax.ppermute(block, axis, [(i, (i + distance) % size) for i in range(size)])


def swapped(block):
    return lax.all_to_all(block, "head", split_axis=0, concat_axis=0, tiled=True)


def crossed(block):
    flat = block.reshape((-1,) + block.shape[2:])
    flat = lax.all_to_all(flat, ("yhi", "head"), split_axis=0, concat_axis=0, tiled=True)
    return flat.reshape(block.shape)


def on_device(query, key, value, out_grad, doc_lengths):
    tokens, heads, width = query.shape
    kv_heads = key.shape[1]
    group = heads // kv_heads

    pair = jnp.transpose(jnp.stack([key, value]), (2, 0, 1, 3))
    pair = crossed(jnp.broadcast_to(pair[None], (QUARTERS // CORES,) + pair.shape))
    both = jnp.stack([query, out_grad]).reshape(2 * tokens, kv_heads, group, width)
    both = jnp.transpose(both, (1, 0, 2, 3))
    pair, both = lax.optimization_barrier((pair, both))
    moved = swapped(both)
    layers = [pair] + [turned(pair, "z", distance) for distance in range(1, SPANS)]
    same_core = jnp.stack(layers)
    other_core = turned(same_core, "core", 1)

    quarter = lax.axis_index("yhi") * CORES + lax.axis_index("core")
    places = jnp.stack([lax.axis_index("z"), quarter]).astype(jnp.int32)
    out_moved, out_window = attention(places, doc_lengths, moved, same_core, other_core)

    back = swapped(out_moved)
    beside = turned(out_window[1].astype(jnp.bfloat16), "core", 1)
    own = out_window[0] + beside.astype(jnp.float32)
    total = own[SPANS - 1]
    for distance in range(SPANS - 1, 0, -1):
        sent = turned(own[SPANS - 1 - distance].astype(jnp.bfloat16), "z", -distance)
        total = total + sent.astype(jnp.float32)
    back, total = lax.optimization_barrier((back, total.astype(jnp.bfloat16)))
    total = crossed(total)
    attended, query_grad = spread(back, query)
    key_grad, value_grad = split(total, key)
    return attended, query_grad, key_grad, value_grad


def solution(mesh):
    ctx, head = mesh.devices.shape
    finer = Mesh(
        mesh.devices.reshape(ctx // QUARTERS, QUARTERS // CORES, CORES, head),
        ("z", "yhi", "core", "head"),
    )
    token_split = P(("z", "yhi", "core", "head"), None, None)
    return jax.shard_map(
        on_device,
        mesh=finer,
        in_specs=(token_split,) * 4 + (P(),),
        out_specs=(token_split,) * 4,
        check_vma=False,
    )
```

```python
import jax
import jax.numpy as jnp
from jax import lax
from jax.experimental import pallas as pl
from jax.experimental.pallas import tpu as pltpu
from jax.sharding import Mesh, PartitionSpec as P

REACH = 8
NEGATIVE = -1e30
LOG2E = 1.4426950408889634
CORES = 2
QUARTERS = 4
SPANS = REACH // QUARTERS + 1


def dot(a, b, dims):
    return lax.dot_general(a, b, (dims, ((), ())), preferred_element_type=jnp.float32)


def attention_kernel(
    places, lengths, moved, same_core, other_core, out_moved, out_window,
    keys, values, keys_t, values_t, key_sum, value_sum, weight_all, dscore_all, ready, sems,
):
    chunks, _, group, width = moved.shape
    chunk_tok = moved.shape[1] // 2
    rows = chunk_tok * group
    block = chunks * chunk_tok
    span = (REACH + 1) * block
    inv_root = width ** (-0.5)
    scale = inv_root * LOG2E
    z_place, quarter = places[0], places[1]
    window_first = (z_place * QUARTERS + quarter - REACH) * block

    for index in range(REACH + 1):
        place = quarter + index
        near, old = lax.rem(place, QUARTERS), SPANS - 1 - lax.div(place, QUARTERS)
        side = lax.div(near, CORES)
        at_home = lax.rem(near, CORES) == lax.rem(quarter, CORES)
        part = pl.ds(index * block, block)
        key_block = jnp.where(
            at_home, same_core[old, side, :, 0], other_core[old, side, :, 0]
        ).reshape(block, width)
        value_block = jnp.where(
            at_home, same_core[old, side, :, 1], other_core[old, side, :, 1]
        ).reshape(block, width)
        keys[part, :] = key_block
        values[part, :] = value_block
        keys_t[:, part] = key_block.T
        values_t[:, part] = value_block.T

    token = lax.broadcasted_iota(jnp.int32, (1, rows), 1) // group

    def first_keys(chunk):
        position = token + (REACH * block + chunk * chunk_tok) + window_first
        begin = jnp.int32(0)
        start = jnp.zeros((1, rows), jnp.int32)
        for doc in range(lengths.shape[0]):
            start = jnp.where(position >= begin, begin, start)
            begin = begin + lengths[doc]
        return start - window_first

    def part_of(index):
        return pl.ds(index * block, block)

    def lanes_of(chunk):
        return pl.ds(chunk * rows, rows)

    def operands(chunk):
        query = moved[chunk, :chunk_tok].reshape(rows, width)
        grad = moved[chunk, chunk_tok:].reshape(rows, width)
        return query, grad

    def live(index, chunk):
        low = chunk * chunk_tok if index == 0 else 0
        high = (chunk + 1) * chunk_tok if index == REACH else block
        return low, high

    def rows_of(index, chunk):
        low, high = live(index, chunk)
        return pl.ds(index * block + low, high - low)

    def clear(held, chunk):
        before, after = chunk * chunk_tok, block - (chunk + 1) * chunk_tok
        if before:
            held[pl.ds(0, before), lanes_of(chunk)] = jnp.zeros((before, rows), held.dtype)
        if after:
            held[pl.ds(span - after, after), lanes_of(chunk)] = jnp.zeros((after, rows), held.dtype)

    state = {}

    def leaving(chunk):
        return pltpu.make_async_copy(ready.at[chunk], out_moved.at[chunk], sems.at[chunk])

    def forward(chunk):
        query, _ = operands(chunk)
        low = first_keys(chunk)
        highest, total, seen = None, None, {}
        for index in [REACH] + list(range(REACH)):
            scores = dot(keys[rows_of(index, chunk), :], query, ((1,), (1,)))
            first, last = live(index, chunk)
            key_row = lax.broadcasted_iota(jnp.int32, (last - first, rows), 0) + first
            allowed = key_row >= low - index * block
            if index == REACH:
                allowed = allowed & (key_row <= token + chunk * chunk_tok)
            scores = jnp.where(allowed, scores, NEGATIVE)
            most = jnp.max(scores, axis=0, keepdims=True)
            if highest is None:
                weights = jnp.exp2((scores - most) * scale)
                total = jnp.sum(weights, axis=0, keepdims=True)
            else:
                most = jnp.maximum(most, highest)
                weights = jnp.exp2((scores - most) * scale)
                total = total * jnp.exp2((highest - most) * scale)
                total = total + jnp.sum(weights, axis=0, keepdims=True)
            highest = most
            seen[index] = most
            weight_all[rows_of(index, chunk), lanes_of(chunk)] = weights.astype(jnp.bfloat16)
            yield
        clear(weight_all, chunk)
        inverse = 1.0 / total
        state[chunk] = {
            index: (jnp.exp2((most - highest) * scale) * inverse).astype(jnp.bfloat16)
            for index, most in seen.items()
        }

    def backward(chunk):
        query, grad = operands(chunk)
        factors = state.pop(chunk)
        for index in range(REACH + 1):
            part = rows_of(index, chunk)
            weight_all[part, lanes_of(chunk)] = weight_all[part, lanes_of(chunk)] * factors[index]
            if index % 3 == 2:
                yield
        attended = dot(values_t[...], weight_all[:, lanes_of(chunk)], ((1,), (0,)))
        attended = attended.astype(jnp.bfloat16)
        ready[chunk, :chunk_tok] = attended.T.reshape(chunk_tok, group, width)
        delta = jnp.sum(
            grad.T.astype(jnp.float32) * attended.astype(jnp.float32), axis=0, keepdims=True
        )
        yield
        for index in range(REACH + 1):
            part = rows_of(index, chunk)
            dprob = dot(values[part, :], grad, ((1,), (1,)))
            slope = (dprob - delta).astype(jnp.bfloat16)
            dscore_all[part, lanes_of(chunk)] = weight_all[part, lanes_of(chunk)] * slope
            yield
        clear(dscore_all, chunk)
        query_grad = dot(keys_t[...], dscore_all[:, lanes_of(chunk)], ((1,), (0,))) * inv_root
        query_grad = query_grad.astype(jnp.bfloat16)
        ready[chunk, chunk_tok:] = query_grad.T.reshape(chunk_tok, group, width)
        leaving(chunk).start()
        yield

    def gather(first, count):
        lanes = pl.ds(first * rows, count * rows)
        chosen = pl.ds(first, count)
        query = moved[chosen, :chunk_tok].reshape(count * rows, width)
        grad = moved[chosen, chunk_tok:].reshape(count * rows, width)
        for index in range(REACH + 1):
            low, high = index * block, (index + 1) * block
            if index == 0:
                low = first * chunk_tok
            if index == REACH:
                high = low + (first + count) * chunk_tok
                if not first:
                    rest = pl.ds(high, span - high)
                    value_sum[rest, :] = jnp.zeros((span - high, width), jnp.float32)
                    key_sum[rest, :] = jnp.zeros((span - high, width), jnp.float32)
            part = pl.ds(low, high - low)
            value_part = dot(weight_all[part, lanes], grad, ((1,), (0,)))
            key_part = dot(dscore_all[part, lanes], query, ((1,), (0,)))
            if first:
                value_part = value_part + value_sum[part, :]
                key_part = key_part + key_sum[part, :]
            value_sum[part, :] = value_part
            key_sum[part, :] = key_part
            if index % 3 == 2:
                yield

    def together(*streams):
        streams = list(streams)
        while streams:
            for stream in list(streams):
                if next(stream, streams) is streams:
                    streams.remove(stream)

    together(forward(0))
    for chunk in range(chunks):
        streams = [backward(chunk)]
        if chunk + 1 < chunks:
            streams.append(forward(chunk + 1))
        if chunk and chunk % 2 == 0:
            streams.append(gather(chunk - 2, 2))
        if chunk == chunks - 1:
            streams.append(gather(chunk - 1, 1))
        together(*streams)
    together(gather(chunks - 1, 1))

    shape = (chunks, chunk_tok, width)
    blank = jnp.zeros((chunks, 2, chunk_tok, width), out_window.dtype)
    for index in range(QUARTERS * SPANS):
        place = lax.rem(quarter + index, QUARTERS * SPANS)
        near, plane = lax.rem(place, QUARTERS), lax.div(place, QUARTERS)
        away = lax.rem(near + quarter, CORES)
        side = lax.div(near, CORES)
        if index <= REACH:
            part = part_of(index)
            out_window[away, plane, side, :, 0] = (key_sum[part, :] * inv_root).reshape(shape)
            out_window[away, plane, side, :, 1] = value_sum[part, :].reshape(shape)
        else:
            out_window[away, plane, side] = blank
    for chunk in range(chunks):
        leaving(chunk).wait()


def attention(places, lengths, moved, same_core, other_core):
    chunks, twice, group, width = moved.shape
    chunk_tok = twice // 2
    block = chunks * chunk_tok
    span = (REACH + 1) * block
    vmem = pl.BlockSpec(memory_space=pltpu.VMEM)
    smem = pl.BlockSpec(memory_space=pltpu.SMEM)
    return pl.pallas_call(
        attention_kernel,
        out_shape=(
            jax.ShapeDtypeStruct(moved.shape, jnp.bfloat16),
            jax.ShapeDtypeStruct((CORES,) + same_core.shape, jnp.float32),
        ),
        in_specs=[smem, smem, vmem, vmem, vmem],
        out_specs=(pl.BlockSpec(memory_space=pl.ANY), vmem),
        scratch_shapes=[
            pltpu.VMEM((span, width), jnp.bfloat16),
            pltpu.VMEM((span, width), jnp.bfloat16),
            pltpu.VMEM((width, span), jnp.bfloat16),
            pltpu.VMEM((width, span), jnp.bfloat16),
            pltpu.VMEM((span, width), jnp.float32),
            pltpu.VMEM((span, width), jnp.float32),
            pltpu.VMEM((span, block * group), jnp.bfloat16),
            pltpu.VMEM((span, block * group), jnp.bfloat16),
            pltpu.VMEM(moved.shape, jnp.bfloat16),
            pltpu.SemaphoreType.DMA((chunks,)),
        ],
        compiler_params=pltpu.CompilerParams(vmem_limit_bytes=40 * 1024 * 1024),
        cost_estimate=pl.CostEstimate(
            flops=12 * block * group * span * width,
            bytes_accessed=4 * moved.size + 4 * same_core.size,
            transcendentals=block * group * span,
        ),
        name="attention",
    )(places, lengths, moved, same_core, other_core)


def spread_kernel(back, attended, query_grad, sems):
    kv_heads, _, group, _ = back.shape
    tokens = attended.shape[0]
    copies = []
    for index in range(kv_heads):
        heads = pl.ds(index * group, group)
        for which, target in enumerate((attended, query_grad)):
            copies.append(
                pltpu.make_async_copy(
                    back.at[index, pl.ds(which * tokens, tokens)],
                    target.at[:, heads, :],
                    sems.at[2 * index + which],
                )
            )
            copies[-1].start()
    for copy in copies:
        copy.wait()


def spread(back, query):
    anywhere = pl.BlockSpec(memory_space=pl.ANY)
    large = jax.ShapeDtypeStruct(query.shape, jnp.bfloat16)
    return pl.pallas_call(
        spread_kernel,
        out_shape=(large, large),
        in_specs=[pl.BlockSpec(memory_space=pltpu.VMEM)],
        out_specs=(anywhere, anywhere),
        scratch_shapes=[pltpu.SemaphoreType.DMA((2 * back.shape[0],))],
        compiler_params=pltpu.CompilerParams(vmem_limit_bytes=16 * 1024 * 1024),
        name="spread",
    )(back)


def split_kernel(total, key_grad, value_grad, spread):
    for which, target in enumerate((key_grad, value_grad)):
        for index in range(total.shape[1]):
            both = total[0, index, which].astype(jnp.float32)
            spread[:, index, :] = both + total[1, index, which].astype(jnp.float32)
        target[...] = spread[...].astype(jnp.bfloat16)


def split(total, key):
    vmem = pl.BlockSpec(memory_space=pltpu.VMEM)
    small = jax.ShapeDtypeStruct(key.shape, jnp.bfloat16)
    return pl.pallas_call(
        split_kernel,
        out_shape=(small, small),
        in_specs=[vmem],
        out_specs=(vmem, vmem),
        scratch_shapes=[pltpu.VMEM(key.shape, jnp.float32)],
        compiler_params=pltpu.CompilerParams(vmem_limit_bytes=16 * 1024 * 1024),
        name="split",
    )(total)


def held_kernel(block, out):
    out[...] = block[...]


def held(block):
    vmem = pl.BlockSpec(memory_space=pltpu.VMEM)
    return pl.pallas_call(
        held_kernel,
        out_shape=jax.ShapeDtypeStruct(block.shape, block.dtype),
        in_specs=[vmem],
        out_specs=vmem,
        cost_estimate=pl.CostEstimate(
            flops=5 * 10**9, bytes_accessed=4 * block.size, transcendentals=0
        ),
        name="held",
    )(block)


def turned(block, axis, distance):
    size = lax.axis_size(axis)
    return lax.ppermute(block, axis, [(i, (i + distance) % size) for i in range(size)])


def swapped(block):
    return lax.all_to_all(block, "head", split_axis=0, concat_axis=0, tiled=True)


def crossed(block):
    flat = block.reshape((-1,) + block.shape[2:])
    flat = lax.all_to_all(flat, ("yhi", "head"), split_axis=0, concat_axis=0, tiled=True)
    return flat.reshape(block.shape)


def on_device(query, key, value, out_grad, doc_lengths):
    tokens, heads, width = query.shape
    kv_heads = key.shape[1]
    group = heads // kv_heads

    pair = jnp.transpose(jnp.stack([key, value]), (2, 0, 1, 3))
    pair = crossed(jnp.broadcast_to(pair[None], (QUARTERS // CORES,) + pair.shape))
    both = jnp.stack([query, out_grad]).reshape(2 * tokens, kv_heads, group, width)
    both = jnp.transpose(both, (1, 0, 2, 3))
    pair, both = lax.optimization_barrier((pair, both))
    moved = swapped(both)
    layers = [pair] + [turned(pair, "z", distance) for distance in range(1, SPANS)]
    layers[-1] = held(layers[-1])
    same_core = jnp.stack(layers)
    other_core = turned(same_core, "core", 1)

    quarter = lax.axis_index("yhi") * CORES + lax.axis_index("core")
    places = jnp.stack([lax.axis_index("z"), quarter]).astype(jnp.int32)
    out_moved, out_window = attention(places, doc_lengths, moved, same_core, other_core)

    back = swapped(out_moved)
    beside = turned(out_window[1].astype(jnp.bfloat16), "core", 1)
    own = out_window[0] + beside.astype(jnp.float32)
    total = own[SPANS - 1]
    for distance in range(SPANS - 1, 0, -1):
        sent = turned(own[SPANS - 1 - distance].astype(jnp.bfloat16), "z", -distance)
        total = total + sent.astype(jnp.float32)
    back, total = lax.optimization_barrier((back, total.astype(jnp.bfloat16)))
    total = crossed(total)
    attended, query_grad = spread(back, query)
    key_grad, value_grad = split(total, key)
    return attended, query_grad, key_grad, value_grad


def solution(mesh):
    ctx, head = mesh.devices.shape
    finer = Mesh(
        mesh.devices.reshape(ctx // QUARTERS, QUARTERS // CORES, CORES, head),
        ("z", "yhi", "core", "head"),
    )
    token_split = P(("z", "yhi", "core", "head"), None, None)
    return jax.shard_map(
        on_device,
        mesh=finer,
        in_specs=(token_split,) * 4 + (P(),),
        out_specs=(token_split,) * 4,
        check_vma=False,
    )
```

```python
import jax
import jax.numpy as jnp
from jax import lax
from jax.experimental import pallas as pl
from jax.experimental.pallas import tpu as pltpu
from jax.sharding import Mesh, PartitionSpec as P

REACH = 8
NEGATIVE = -1e30
LOG2E = 1.4426950408889634
CORES = 2
QUARTERS = 4
SPANS = REACH // QUARTERS + 1


def dot(a, b, dims):
    return lax.dot_general(a, b, (dims, ((), ())), preferred_element_type=jnp.float32)


def attention_kernel(
    places, lengths, moved, same_core, other_core, out_moved, out_window,
    keys, values, keys_t, values_t, key_sum, value_sum, weight_all, dscore_all, ready, sems,
):
    chunks, _, group, width = moved.shape
    chunk_tok = moved.shape[1] // 2
    rows = chunk_tok * group
    block = chunks * chunk_tok
    span = (REACH + 1) * block
    inv_root = width ** (-0.5)
    scale = inv_root * LOG2E
    z_place, quarter = places[0], places[1]
    window_first = (z_place * QUARTERS + quarter - REACH) * block

    for index in range(REACH + 1):
        place = quarter + index
        near, old = lax.rem(place, QUARTERS), SPANS - 1 - lax.div(place, QUARTERS)
        side = lax.div(near, CORES)
        at_home = lax.rem(near, CORES) == lax.rem(quarter, CORES)
        part = pl.ds(index * block, block)
        key_block = jnp.where(
            at_home, same_core[old, side, :, 0], other_core[old, side, :, 0]
        ).reshape(block, width)
        value_block = jnp.where(
            at_home, same_core[old, side, :, 1], other_core[old, side, :, 1]
        ).reshape(block, width)
        keys[part, :] = key_block
        values[part, :] = value_block
        keys_t[:, part] = key_block.T
        values_t[:, part] = value_block.T

    token = lax.broadcasted_iota(jnp.int32, (1, rows), 1) // group

    def first_keys(chunk):
        position = token + (REACH * block + chunk * chunk_tok) + window_first
        begin = jnp.int32(0)
        start = jnp.zeros((1, rows), jnp.int32)
        for doc in range(lengths.shape[0]):
            start = jnp.where(position >= begin, begin, start)
            begin = begin + lengths[doc]
        return start - window_first

    def part_of(index):
        return pl.ds(index * block, block)

    def lanes_of(chunk):
        return pl.ds(chunk * rows, rows)

    def operands(chunk):
        query = moved[chunk, :chunk_tok].reshape(rows, width)
        grad = moved[chunk, chunk_tok:].reshape(rows, width)
        return query, grad

    def live(index, chunk):
        low = chunk * chunk_tok if index == 0 else 0
        high = (chunk + 1) * chunk_tok if index == REACH else block
        return low, high

    def rows_of(index, chunk):
        low, high = live(index, chunk)
        return pl.ds(index * block + low, high - low)

    def clear(held, chunk):
        before, after = chunk * chunk_tok, block - (chunk + 1) * chunk_tok
        if before:
            held[pl.ds(0, before), lanes_of(chunk)] = jnp.zeros((before, rows), held.dtype)
        if after:
            held[pl.ds(span - after, after), lanes_of(chunk)] = jnp.zeros((after, rows), held.dtype)

    def three_blocks(held, right, first, chunk):
        low = first * block + live(first, chunk)[0]
        high = (first + 2) * block + live(first + 2, chunk)[1]
        result = dot(held[pl.ds(low, high - low), :], right, ((1,), (0,)))
        pieces = {}
        for index in range(first, first + 3):
            start, stop = live(index, chunk)
            pieces[index] = result[index * block + start - low : index * block + stop - low]
        return pieces

    state = {}

    def leaving(chunk):
        return pltpu.make_async_copy(ready.at[chunk], out_moved.at[chunk], sems.at[chunk])

    def forward(chunk):
        query_t = operands(chunk)[0].T
        low = first_keys(chunk)
        pieces = {}
        highest, total, seen = None, None, {}
        for index in [REACH, REACH - 1, REACH - 2] + list(range(REACH - 2)):
            if index not in pieces:
                pieces = three_blocks(keys, query_t, index - index % 3, chunk)
            scores = pieces[index]
            first, last = live(index, chunk)
            key_row = lax.broadcasted_iota(jnp.int32, (last - first, rows), 0) + first
            allowed = key_row >= low - index * block
            if index == REACH:
                allowed = allowed & (key_row <= token + chunk * chunk_tok)
            scores = jnp.where(allowed, scores, NEGATIVE)
            most = jnp.max(scores, axis=0, keepdims=True)
            if highest is None:
                weights = jnp.exp2((scores - most) * scale)
                total = jnp.sum(weights, axis=0, keepdims=True)
            else:
                most = jnp.maximum(most, highest)
                weights = jnp.exp2((scores - most) * scale)
                total = total * jnp.exp2((highest - most) * scale)
                total = total + jnp.sum(weights, axis=0, keepdims=True)
            highest = most
            seen[index] = most
            weight_all[rows_of(index, chunk), lanes_of(chunk)] = weights.astype(jnp.bfloat16)
            yield
        clear(weight_all, chunk)
        inverse = 1.0 / total
        state[chunk] = {
            index: (jnp.exp2((most - highest) * scale) * inverse).astype(jnp.bfloat16)
            for index, most in seen.items()
        }

    def backward(chunk):
        grad_t = operands(chunk)[1].T
        factors = state.pop(chunk)
        for index in range(REACH + 1):
            part = rows_of(index, chunk)
            weight_all[part, lanes_of(chunk)] = weight_all[part, lanes_of(chunk)] * factors[index]
            if index % 3 == 2:
                yield
        attended = dot(values_t[...], weight_all[:, lanes_of(chunk)], ((1,), (0,)))
        attended = attended.astype(jnp.bfloat16)
        ready[chunk, :chunk_tok] = attended.T.reshape(chunk_tok, group, width)
        delta = jnp.sum(
            grad_t.astype(jnp.float32) * attended.astype(jnp.float32), axis=0, keepdims=True
        )
        yield
        for index in range(REACH + 1):
            part = rows_of(index, chunk)
            if index % 3 == 0:
                pieces = three_blocks(values, grad_t, index, chunk)
            slope = (pieces[index] - delta).astype(jnp.bfloat16)
            dscore_all[part, lanes_of(chunk)] = weight_all[part, lanes_of(chunk)] * slope
            yield
        clear(dscore_all, chunk)
        query_grad = dot(keys_t[...], dscore_all[:, lanes_of(chunk)], ((1,), (0,))) * inv_root
        query_grad = query_grad.astype(jnp.bfloat16)
        ready[chunk, chunk_tok:] = query_grad.T.reshape(chunk_tok, group, width)
        leaving(chunk).start()
        yield

    def gather(first, count):
        lanes = pl.ds(first * rows, count * rows)
        chosen = pl.ds(first, count)
        query = moved[chosen, :chunk_tok].reshape(count * rows, width)
        grad = moved[chosen, chunk_tok:].reshape(count * rows, width)
        for index in range(REACH + 1):
            low, high = index * block, (index + 1) * block
            if index == 0:
                low = first * chunk_tok
            if index == REACH:
                high = low + (first + count) * chunk_tok
                if not first:
                    rest = pl.ds(high, span - high)
                    value_sum[rest, :] = jnp.zeros((span - high, width), jnp.float32)
                    key_sum[rest, :] = jnp.zeros((span - high, width), jnp.float32)
            part = pl.ds(low, high - low)
            value_part = dot(weight_all[part, lanes], grad, ((1,), (0,)))
            key_part = dot(dscore_all[part, lanes], query, ((1,), (0,)))
            if first:
                value_part = value_part + value_sum[part, :]
                key_part = key_part + key_sum[part, :]
            value_sum[part, :] = value_part
            key_sum[part, :] = key_part
            if index % 3 == 2:
                yield

    def together(*streams):
        streams = list(streams)
        while streams:
            for stream in list(streams):
                if next(stream, streams) is streams:
                    streams.remove(stream)

    together(forward(0))
    for chunk in range(chunks):
        streams = [backward(chunk)]
        if chunk + 1 < chunks:
            streams.append(forward(chunk + 1))
        if chunk and chunk % 2 == 0:
            streams.append(gather(chunk - 2, 2))
        if chunk == chunks - 1:
            streams.append(gather(chunk - 1, 1))
        together(*streams)
    together(gather(chunks - 1, 1))

    shape = (chunks, chunk_tok, width)
    blank = jnp.zeros((chunks, 2, chunk_tok, width), out_window.dtype)
    for index in range(QUARTERS * SPANS):
        place = lax.rem(quarter + index, QUARTERS * SPANS)
        near, plane = lax.rem(place, QUARTERS), lax.div(place, QUARTERS)
        away = lax.rem(near + quarter, CORES)
        side = lax.div(near, CORES)
        if index <= REACH:
            part = part_of(index)
            out_window[away, plane, side, :, 0] = (key_sum[part, :] * inv_root).reshape(shape)
            out_window[away, plane, side, :, 1] = value_sum[part, :].reshape(shape)
        else:
            out_window[away, plane, side] = blank
    for chunk in range(chunks):
        leaving(chunk).wait()


def attention(places, lengths, moved, same_core, other_core):
    chunks, twice, group, width = moved.shape
    chunk_tok = twice // 2
    block = chunks * chunk_tok
    span = (REACH + 1) * block
    vmem = pl.BlockSpec(memory_space=pltpu.VMEM)
    smem = pl.BlockSpec(memory_space=pltpu.SMEM)
    return pl.pallas_call(
        attention_kernel,
        out_shape=(
            jax.ShapeDtypeStruct(moved.shape, jnp.bfloat16),
            jax.ShapeDtypeStruct((CORES,) + same_core.shape, jnp.float32),
        ),
        in_specs=[smem, smem, vmem, vmem, vmem],
        out_specs=(pl.BlockSpec(memory_space=pl.ANY), vmem),
        scratch_shapes=[
            pltpu.VMEM((span, width), jnp.bfloat16),
            pltpu.VMEM((span, width), jnp.bfloat16),
            pltpu.VMEM((width, span), jnp.bfloat16),
            pltpu.VMEM((width, span), jnp.bfloat16),
            pltpu.VMEM((span, width), jnp.float32),
            pltpu.VMEM((span, width), jnp.float32),
            pltpu.VMEM((span, block * group), jnp.bfloat16),
            pltpu.VMEM((span, block * group), jnp.bfloat16),
            pltpu.VMEM(moved.shape, jnp.bfloat16),
            pltpu.SemaphoreType.DMA((chunks,)),
        ],
        compiler_params=pltpu.CompilerParams(vmem_limit_bytes=40 * 1024 * 1024),
        cost_estimate=pl.CostEstimate(
            flops=12 * block * group * span * width,
            bytes_accessed=4 * moved.size + 4 * same_core.size,
            transcendentals=block * group * span,
        ),
        name="attention",
    )(places, lengths, moved, same_core, other_core)


def spread_kernel(back, attended, query_grad, sems):
    kv_heads, _, group, _ = back.shape
    tokens = attended.shape[0]
    copies = []
    for index in range(kv_heads):
        heads = pl.ds(index * group, group)
        for which, target in enumerate((attended, query_grad)):
            copies.append(
                pltpu.make_async_copy(
                    back.at[index, pl.ds(which * tokens, tokens)],
                    target.at[:, heads, :],
                    sems.at[2 * index + which],
                )
            )
            copies[-1].start()
    for copy in copies:
        copy.wait()


def spread(back, query):
    anywhere = pl.BlockSpec(memory_space=pl.ANY)
    large = jax.ShapeDtypeStruct(query.shape, jnp.bfloat16)
    return pl.pallas_call(
        spread_kernel,
        out_shape=(large, large),
        in_specs=[pl.BlockSpec(memory_space=pltpu.VMEM)],
        out_specs=(anywhere, anywhere),
        scratch_shapes=[pltpu.SemaphoreType.DMA((2 * back.shape[0],))],
        compiler_params=pltpu.CompilerParams(vmem_limit_bytes=16 * 1024 * 1024),
        name="spread",
    )(back)


def split_kernel(total, key_grad, value_grad, spread):
    for which, target in enumerate((key_grad, value_grad)):
        for index in range(total.shape[1]):
            both = total[0, index, which].astype(jnp.float32)
            spread[:, index, :] = both + total[1, index, which].astype(jnp.float32)
        target[...] = spread[...].astype(jnp.bfloat16)


def split(total, key):
    vmem = pl.BlockSpec(memory_space=pltpu.VMEM)
    small = jax.ShapeDtypeStruct(key.shape, jnp.bfloat16)
    return pl.pallas_call(
        split_kernel,
        out_shape=(small, small),
        in_specs=[vmem],
        out_specs=(vmem, vmem),
        scratch_shapes=[pltpu.VMEM(key.shape, jnp.float32)],
        compiler_params=pltpu.CompilerParams(vmem_limit_bytes=16 * 1024 * 1024),
        name="split",
    )(total)


def turned(block, axis, distance):
    size = lax.axis_size(axis)
    return lax.ppermute(block, axis, [(i, (i + distance) % size) for i in range(size)])


def swapped(block):
    return lax.all_to_all(block, "head", split_axis=0, concat_axis=0, tiled=True)


def crossed(block):
    flat = block.reshape((-1,) + block.shape[2:])
    flat = lax.all_to_all(flat, ("yhi", "head"), split_axis=0, concat_axis=0, tiled=True)
    return flat.reshape(block.shape)


def on_device(query, key, value, out_grad, doc_lengths):
    tokens, heads, width = query.shape
    kv_heads = key.shape[1]
    group = heads // kv_heads

    pair = jnp.transpose(jnp.stack([key, value]), (2, 0, 1, 3))
    pair = crossed(jnp.broadcast_to(pair[None], (QUARTERS // CORES,) + pair.shape))
    both = jnp.stack([query, out_grad]).reshape(2 * tokens, kv_heads, group, width)
    both = jnp.transpose(both, (1, 0, 2, 3))
    pair, both = lax.optimization_barrier((pair, both))
    moved = swapped(both)
    layers = [pair] + [turned(pair, "z", distance) for distance in range(1, SPANS)]
    same_core = jnp.stack(layers)
    other_core = turned(same_core, "core", 1)

    quarter = lax.axis_index("yhi") * CORES + lax.axis_index("core")
    places = jnp.stack([lax.axis_index("z"), quarter]).astype(jnp.int32)
    out_moved, out_window = attention(places, doc_lengths, moved, same_core, other_core)

    back = swapped(out_moved)
    beside = turned(out_window[1].astype(jnp.bfloat16), "core", 1)
    own = out_window[0] + beside.astype(jnp.float32)
    total = own[SPANS - 1]
    for distance in range(SPANS - 1, 0, -1):
        sent = turned(own[SPANS - 1 - distance].astype(jnp.bfloat16), "z", -distance)
        total = total + sent.astype(jnp.float32)
    back, total = lax.optimization_barrier((back, total.astype(jnp.bfloat16)))
    total = crossed(total)
    attended, query_grad = spread(back, query)
    key_grad, value_grad = split(total, key)
    return attended, query_grad, key_grad, value_grad


def solution(mesh):
    ctx, head = mesh.devices.shape
    finer = Mesh(
        mesh.devices.reshape(ctx // QUARTERS, QUARTERS // CORES, CORES, head),
        ("z", "yhi", "core", "head"),
    )
    token_split = P(("z", "yhi", "core", "head"), None, None)
    return jax.shard_map(
        on_device,
        mesh=finer,
        in_specs=(token_split,) * 4 + (P(),),
        out_specs=(token_split,) * 4,
        check_vma=False,
    )
```
